128 devices in a mesh: pole: 8 (over x, z_lo), col: 16 (over z_hi, y, core).
Axes of the slice: x: 4, y: 4, z: 4 (z_hi: 2, z_lo: 2; z = z_hi * 2 + z_lo), core: 2. Of those that a mesh axis runs over, the one named last changes fastest.
Arguments:
- panel: bfloat16 [256, 3072, 128], P('col', 'pole'), may hold values from -36 to 36
- pivot_inverse: bfloat16 [8, 256, 128, 128], P('pole', 'col'), may hold values from -0.5 to 0.5
- row_count: int32 [256], replicated, may hold values from 1 to 24, 3072 in all
- pole_weight: float32 [8], replicated, may hold values from 0.25 to 2
Outputs:
- density_panel: bfloat16 [256, 3072, 128], P('col', 'pole')
- density_diag: bfloat16 [256, 128, 128], P('col', 'pole')
The draws below stay inside these ranges and needn't reach their ends.
All inputs are finite; a program needn't handle non-finite values.
Results may differ from the reference program's by a relative error of at most 0.017.
Values may be sent and summed in bfloat16 or wider, within the bound.
No kernel may reach another device: no remote copies, remote signals or barrier semaphores. Data moves between devices by JAX's collectives and lax.ppermute only.
A program may use at most 128 MiB of HBM per device.

```python
import math
import jax
import jax.numpy as jnp
import numpy as np
from jax import lax

BLOCK = 128
SUPER_DEV = 16
ROWB = 24
ROWB_DEV = 3
SUPER = 256
POLES = 8
N_POLE = 8
N_COL = 16


def draw_panel(key, part):
    key = jax.random.fold_in(key, 7)
    first, second, third = jax.random.split(key, 3)
    shape = (SUPER, ROWB * BLOCK, BLOCK)
    row_scale = jnp.exp(jax.random.uniform(first, (SUPER, ROWB * BLOCK, 1), jnp.float32, math.log(0.3), math.log(3.0)))
    col_scale = jnp.exp(jax.random.uniform(second, (SUPER, 1, BLOCK), jnp.float32, math.log(0.3), math.log(3.0)))
    values = jax.random.truncated_normal(third, -4.0, 4.0, shape, jnp.float32)
    return (row_scale * col_scale * values).astype(jnp.bfloat16)


def shard_levels(rng, shape, shards, smallest, largest):
    level = 1.0
    for position, parts in shards:
        steps = jax.random.uniform(jax.random.fold_in(jax.random.fold_in(rng, 6), position), (parts,), jnp.float32, smallest / len(shards), largest / len(shards))
        level = level * jnp.repeat(jnp.exp(steps), shape[position] // parts).reshape((-1,) + (1,) * (len(shape) - 1 - position))
    return level


def split_up(number_of, total, bound, skew):
    weights = [(1 << 20) // math.isqrt(rank ** skew) + 1 for rank in range(2, number_of + 1)]
    surplus, holding = total - bound - (number_of - 1), [1] * (number_of - 1)
    while surplus > 0:
        candidates = [i for i in range(number_of - 1) if holding[i] < bound]
        pool, left = sum([weights[i] for i in candidates]), surplus
        for i in candidates:
            more = min(bound - holding[i], max(1, left * weights[i] // pool), surplus)
            holding[i] = holding[i] + more
            surplus = surplus - more
    return np.array([bound] + holding)


def ragged_sizes(key, number_of, total, reach, lean):
    if number_of == 2:
        one = jax.random.randint(key, (), max(1, total - reach), min(reach, total - 1) + 1)
        return jnp.stack([one, total - one])
    tallies = jnp.asarray(split_up(number_of, total, reach, lean), jnp.int32)
    twos = (number_of - 1) // 2
    donor, receiver = tallies[1:1 + 2 * twos:2], tallies[2:2 + 2 * twos:2]
    room = jnp.minimum(donor - 1, reach - receiver)
    passed = jax.random.randint(jax.random.fold_in(key, 1), (twos,), 0, 1 << 20) % (room + 1)
    tallies = tallies.at[1:1 + 2 * twos:2].set(donor - passed).at[2:2 + 2 * twos:2].set(receiver + passed)
    return tallies[jax.random.permutation(jax.random.fold_in(key, 2), number_of)]


def bell_draw(stream_key, dims, spread, most, pieces=(), kind=jnp.bfloat16):
    values = jax.random.normal(stream_key, dims, jnp.float32) * spread
    if len(pieces) > 0:
        values = shard_levels(stream_key, dims, pieces, -0.22, 0.18) * values
    return jnp.clip(values, min=-most, max=most).astype(kind)


def setup_inputs(seed: int = 0) -> dict:
    streams_of = jax.random.split(jax.random.key(seed), 5)
    panel = draw_panel(jax.random.fold_in(streams_of[4], 71), 0)
    pivot_inverse = bell_draw(streams_of[1], (POLES, SUPER, BLOCK, BLOCK), BLOCK ** -0.5, 0.5, ((0, 8), (1, 16)))
    row_count = ragged_sizes(streams_of[2], SUPER, SUPER * ROWB // 2, ROWB, 2).astype(jnp.int32)
    pole_weight = jnp.clip(jnp.exp(jax.random.uniform(streams_of[3], (POLES,), jnp.float32, math.log(0.25), math.log(2.0))), 0.25, 2.0)
    return {"panel": panel, "pivot_inverse": pivot_inverse, "row_count": row_count, "pole_weight": pole_weight}


def rounded_back(values):
    return lax.optimization_barrier(values.astype(jnp.bfloat16)).astype(jnp.float32)


def reference(panel, pivot_inverse, row_count, pole_weight):
    by_super = panel.reshape(N_COL, SUPER_DEV, ROWB * BLOCK, BLOCK).transpose(1, 0, 2, 3)
    by_super = by_super.reshape(SUPER, N_POLE, ROWB_DEV, BLOCK, BLOCK).transpose(0, 2, 1, 3, 4)
    row_index = jnp.arange(ROWB, dtype=jnp.int32)
    keep = (row_index[None, :] < row_count[:, None]).astype(jnp.bfloat16)
    natural = (by_super.reshape(SUPER, ROWB, BLOCK, BLOCK) * keep[:, :, None, None]).reshape(SUPER, ROWB * BLOCK, BLOCK)
    row_total = (BLOCK * row_count).astype(jnp.float32)
    inverses = pivot_inverse.transpose(1, 0, 2, 3)

    def one_super(items):
        block_panel, inverse, total = items
        panel_sum = jnp.zeros((ROWB * BLOCK, BLOCK), jnp.float32)
        diag_sum = jnp.zeros((BLOCK, BLOCK), jnp.float32)
        for index in range(POLES):
            product = jnp.dot(block_panel, inverse[index], preferred_element_type=jnp.float32)
            frontal = lax.optimization_barrier(product.astype(jnp.bfloat16))
            gram = jnp.dot(frontal.T, frontal, preferred_element_type=jnp.float32)
            panel_sum = panel_sum + rounded_back(-pole_weight[index] * frontal.astype(jnp.float32))
            diag_sum = diag_sum + pole_weight[index] * (inverse[index].astype(jnp.float32) + gram / total)
        return panel_sum.astype(jnp.bfloat16), diag_sum.astype(jnp.bfloat16)

    panel_out, diag_out = lax.map(one_super, (natural, inverses, row_total))
    panel_out = panel_out.reshape(SUPER, ROWB_DEV, N_POLE, BLOCK, BLOCK).transpose(0, 2, 1, 3, 4)
    return panel_out.reshape(SUPER, ROWB * BLOCK, BLOCK), diag_out
```

```python
import jax
import jax.numpy as jnp
from jax import lax
from jax.sharding import PartitionSpec as P


def shards(panel, pivot_inverse, row_count, pole_weight):
    owned, rows, block = panel.shape
    rows_local = rows // block
    poles = lax.axis_size("pole")
    cols = lax.axis_size("col")
    pole_at = lax.axis_index("pole")
    col_at = lax.axis_index("col")
    share = owned // poles
    moved = lax.all_to_all(panel, "col", 0, 0, tiled=True)
    natural_row = jnp.arange(rows_local, dtype=jnp.int32) * poles + pole_at
    stored_counts = lax.dynamic_index_in_dim(row_count.reshape(owned, cols), col_at, 1, keepdims=False)
    keep = (natural_row[None, :] < stored_counts[:, None]).astype(jnp.bfloat16)
    masked = (panel.reshape(owned, rows_local, block, block) * keep[:, :, None, None]).reshape(owned, rows, block)
    part = jnp.einsum("sra,srb->sab", masked, masked, preferred_element_type=jnp.float32).astype(jnp.bfloat16)
    sent = jnp.stack([pivot_inverse[0], part], axis=1)
    got = lax.all_to_all(sent, "pole", 0, 0, tiled=True).reshape(poles, share, 2, block, block)
    inv = got[:, :, 0]
    gram = jnp.sum(got[:, :, 1].astype(jnp.float32), axis=0)
    w = pole_weight
    msum = jnp.einsum("p,psab->sab", w, inv.astype(jnp.float32), precision="highest")
    mneg = (-msum).astype(jnp.bfloat16)
    mall = lax.all_gather(mneg, "pole", axis=0, tiled=True)
    half = lax.rem(col_at, 2)
    a = lax.dynamic_index_in_dim(gram, half, 0, keepdims=False)
    b = lax.dynamic_index_in_dim(gram, 1 - half, 0, keepdims=False)
    n = poles * cols
    sw = lambda p, c, f: (c // 2) * cols + 2 * p + ((c % 2) ^ f)
    pa = [(p * cols + c, sw(p, c, 0)) for p in range(poles) for c in range(cols)]
    pb = [(p * cols + c, sw(p, c, 1)) for p in range(poles) for c in range(cols)]
    a = lax.ppermute(a, ("pole", "col"), pa)
    b = lax.ppermute(b, ("pole", "col"), pb)
    lo = jnp.where(half == 0, a, b)
    hi = jnp.where(half == 0, b, a)
    full = jnp.stack([lo, hi])
    mine = lax.dynamic_slice_in_dim(row_count, col_at * owned + pole_at * share, share, 0)
    scale = 1.0 / (block * mine).astype(jnp.float32)
    inv32 = inv.astype(jnp.float32)
    right = jnp.einsum("sab,psbc->psac", full, inv32, precision="highest")
    quad = jnp.einsum("psab,psac->sbc", inv32 * w[:, None, None, None], right, precision="highest")
    diag = (msum + quad * scale[:, None, None]).astype(jnp.bfloat16)
    diag = lax.all_to_all(diag, "pole", 1, 0, tiled=True)
    counts = lax.dynamic_slice_in_dim(row_count, col_at * owned, owned, 0)
    keep2 = (natural_row[None, :] < counts[:, None]).astype(jnp.bfloat16)
    masked2 = (moved.reshape(owned, rows_local, block, block) * keep2[:, :, None, None]).reshape(owned, rows, block)
    density = jnp.einsum("srk,skj->srj", masked2, mall, preferred_element_type=jnp.float32).astype(jnp.bfloat16)
    return density, diag


def solution(mesh):
    placed = (P("col", "pole", None), P("pole", "col", None, None), P(), P())
    return jax.shard_map(
        shards,
        mesh=mesh,
        in_specs=placed,
        out_specs=(P("col", "pole", None), P("col", "pole", None)),
        check_vma=False,
    )
```

```python
import functools

import jax
import jax.numpy as jnp
from jax import lax
from jax.experimental import pallas as pl
from jax.experimental.pallas import tpu as pltpu
from jax.sharding import PartitionSpec as P

F32 = jnp.float32
BF16 = jnp.bfloat16


def dot(a, b):
    return lax.dot_general(a, b, (((1,), (0,)), ((), ())), preferred_element_type=F32)


def dot_t(a, b):
    return lax.dot_general(a, b, (((0,), (0,)), ((), ())), preferred_element_type=F32)


def kept_rows(source, count, pole, poles, block):
    zero = jnp.zeros((block, block), BF16)
    rows_local = source.shape[0] // block
    return jnp.concatenate(
        [
            lax.select(k * poles + pole < count, source[pl.ds(k * block, block), :], zero)
            for k in range(rows_local)
        ],
        axis=0,
    )


def gram_kernel(poles, share, at_ref, count_ref, panel_ref, inv_ref, *out_refs):
    pole, col = at_ref[0], at_ref[1]
    owned, block = inv_ref.shape[0], inv_ref.shape[1]
    for k, out_ref in enumerate(out_refs):
        for t in range(share):
            i = col ^ (share * ((pole // 2) ^ k) + t)
            x = kept_rows(panel_ref.at[i], count_ref[i * owned + col], pole, poles, block)
            out_ref[t, 0] = inv_ref[i]
            out_ref[t, 1] = dot_t(x, x).astype(BF16)


def sums_kernel(share, at_ref, w_ref, *refs):
    *got_refs, m_ref, g_ref = refs
    pole = at_ref[0]
    for t in range(share):
        m = g = None
        for k, got_ref in enumerate(got_refs):
            mk = -w_ref[pole ^ (2 * k)] * got_ref[t, 0].astype(F32)
            gk = got_ref[t, 1].astype(F32)
            m, g = (mk, gk) if m is None else (m + mk, g + gk)
        m_ref[t] = m.astype(BF16)
        g_ref[t] = g.astype(BF16)


def both_kernel(a_ref, b_ref, *out_refs):
    for t, out_ref in enumerate(out_refs):
        out_ref[...] = (a_ref[t].astype(F32) + b_ref[t].astype(F32)).astype(BF16)


def add_kernel(a_ref, b_ref, out_ref):
    out_ref[...] = (a_ref[...].astype(F32) + b_ref[...].astype(F32)).astype(BF16)


def diag_kernel(share, at_ref, count_ref, w_ref, *refs):
    half = (len(refs) - 1 - share)
    g_refs, got_refs, out_ref = refs[:share], refs[share:share + half], refs[-1]
    pole, col = at_ref[0], at_ref[1]
    owned = share * half
    block = g_refs[0].shape[0]
    chunk = out_ref.shape[2]
    for t in range(share):
        count = count_ref[col * owned + (col ^ (share * (pole // 2) + t))]
        scale = 1.0 / (jnp.full((block, block), block, F32) * count.astype(F32))
        g = g_refs[t][...]
        acc = jnp.zeros((block, block), F32)
        base = jnp.zeros((block, block), F32)
        for k in range(half):
            inv = got_refs[k][t, 0]
            w = w_ref[pole ^ (2 * k)]
            v = w * dot(g, inv)
            hi = v.astype(BF16)
            lo = (v - hi.astype(F32)).astype(BF16)
            acc = acc + dot_t(inv, hi) + dot_t(inv, lo)
            base = base + w * inv.astype(F32)
        d = (base + acc * scale).astype(BF16)
        for p in range(out_ref.shape[0]):
            out_ref[p, t] = d[p * chunk:(p + 1) * chunk]


def finish_kernel(share, at_ref, got_ref, out_ref):
    col = at_ref[1]
    for x in range(got_ref.shape[0] // 2):
        for t in range(share):
            d = got_ref[2 * x, t].astype(F32) + got_ref[2 * x + 1, t].astype(F32)
            out_ref[col ^ (share * x + t)] = d.astype(BF16)


def density_kernel(poles, share, at_ref, count_ref, moved_ref, *refs):
    *m_refs, out_ref = refs
    pole, col = at_ref[0], at_ref[1]
    owned, block = moved_ref.shape[0], moved_ref.shape[2]
    for k, m_ref in enumerate(m_refs):
        for t in range(share):
            i = col ^ (share * ((pole // 2) ^ k) + t)
            x = kept_rows(moved_ref.at[i], count_ref[col * owned + i], pole, poles, block)
            out_ref[i] = dot(x, m_ref[t]).astype(BF16)


def shards(panel, pivot_inverse, row_count, pole_weight):
    owned, rows, block = panel.shape
    poles = lax.axis_size("pole")
    cols = lax.axis_size("col")
    pole_at = lax.axis_index("pole")
    col_at = lax.axis_index("col")
    half = poles // 2
    share = owned // half
    chunk = block // poles
    at = jnp.stack([pole_at, col_at]).astype(jnp.int32)
    smem = pl.BlockSpec(memory_space=pltpu.SMEM)
    vmem = pl.BlockSpec(memory_space=pltpu.VMEM)
    shape = lambda *s: jax.ShapeDtypeStruct(s, BF16)

    def call(body, name, ins, outs, flops=0):
        moved_bytes = 2 * sum(o.size for o in outs) * 2
        return pl.pallas_call(
            body,
            in_specs=ins,
            out_specs=[vmem] * len(outs),
            out_shape=outs,
            compiler_params=pltpu.CompilerParams(vmem_limit_bytes=32 * 1024 * 1024),
            cost_estimate=pl.CostEstimate(flops=flops, bytes_accessed=moved_bytes, transcendentals=0),
            name=name,
        )

    def swap(x, k):
        return lax.ppermute(x, "pole", [(i, i ^ k) for i in range(poles)])

    moved = lax.all_to_all(panel, "col", 0, 0, tiled=True)

    sent = call(
        functools.partial(gram_kernel, poles, share), "gram",
        [smem, smem, vmem, vmem], [shape(share, 2, block, block)] * half,
        2 * owned * rows * block * block,
    )(at, row_count, panel, pivot_inverse[0])
    got = [sent[0]] + [swap(sent[k], 2 * k) for k in range(1, half)]
    mhalf, ghalf = call(
        functools.partial(sums_kernel, share), "sums",
        [smem, smem] + [vmem] * half, [shape(share, block, block)] * 2,
    )(at, pole_weight, *got)

    grams = call(both_kernel, "grams", [vmem] * 2, [shape(block, block)] * share)(ghalf, swap(ghalf, 1))

    def to_owner(g, t):
        return lax.ppermute(
            g, ("pole", "col"),
            [(p * cols + c, p * cols + (c ^ (share * (p // 2) + t))) for p in range(poles) for c in range(cols)],
        )

    grams = [to_owner(g, t) for t, g in enumerate(grams)]
    mfull = call(add_kernel, "weights", [vmem] * 2, [shape(share, block, block)])(mhalf, swap(mhalf, 1))[0]
    mparts = [mfull] + [swap(mfull, 2 * k) for k in range(1, half)]

    part = call(
        functools.partial(diag_kernel, share), "diag",
        [smem, smem, smem] + [vmem] * (share + half), [shape(poles, share, chunk, block)],
        6 * owned * block * block * block,
    )(at, row_count, pole_weight, *grams, *got)[0]
    part, moved = lax.optimization_barrier((part, moved))
    part = lax.all_to_all(part, "pole", 0, 0, tiled=True)
    diag = call(functools.partial(finish_kernel, share), "finish", [smem, vmem], [shape(owned, chunk, block)])(at, part)[0]

    density = call(
        functools.partial(density_kernel, poles, share), "density",
        [smem, smem, vmem] + [vmem] * half, [shape(owned, rows, block)],
        2 * owned * rows * block * block,
    )(at, row_count, moved, *mparts)[0]
    return density, diag


def solution(mesh):
    placed = (P("col", "pole", None), P("pole", "col", None, None), P(), P())
    return jax.shard_map(
        shards,
        mesh=mesh,
        in_specs=placed,
        out_specs=(P("col", "pole", None), P("col", "pole", None)),
        check_vma=False,
    )
```

```python
import functools

import jax
import jax.numpy as jnp
from jax import lax
from jax.experimental import pallas as pl
from jax.experimental.pallas import tpu as pltpu
from jax.sharding import PartitionSpec as P

F32 = jnp.float32
BF16 = jnp.bfloat16


def dot(a, b):
    return lax.dot_general(a, b, (((1,), (0,)), ((), ())), preferred_element_type=F32)


def dot_t(a, b):
    return lax.dot_general(a, b, (((0,), (0,)), ((), ())), preferred_element_type=F32)


def kept_rows(source, count, pole, poles, block):
    zero = jnp.zeros((block, block), BF16)
    rows_local = source.shape[0] // block
    return jnp.concatenate(
        [
            lax.select(k * poles + pole < count, source[pl.ds(k * block, block), :], zero)
            for k in range(rows_local)
        ],
        axis=0,
    )


def gram_kernel(poles, share, at_ref, count_ref, panel_ref, inv_ref, *out_refs):
    pole, col = at_ref[0], at_ref[1]
    owned, block = inv_ref.shape[0], inv_ref.shape[1]
    half = len(out_refs) // 2
    for k in range(half):
        for t in range(share):
            i = col ^ (share * ((pole // 2) ^ k) + t)
            x = kept_rows(panel_ref.at[i], count_ref[i * owned + col], pole, poles, block)
            out_refs[k][t] = dot_t(x, x).astype(BF16)
            out_refs[half + k][t] = inv_ref[i]


def gsum_kernel(share, *refs):
    *got_refs, keep_ref, give_ref = refs
    for t in range(share):
        g = sum(got_ref[t].astype(F32) for got_ref in got_refs).astype(BF16)
        (give_ref if t % 2 else keep_ref)[t // 2] = g


def pair_kernel(a_ref, b_ref, out_ref):
    out_ref[:, 0] = a_ref[...]
    out_ref[:, 1] = b_ref[...]


def both_kernel(a_ref, b_ref, *out_refs):
    for t, out_ref in enumerate(out_refs):
        out_ref[...] = (a_ref[t].astype(F32) + b_ref[t].astype(F32)).astype(BF16)


def add_kernel(a_ref, b_ref, out_ref):
    out_ref[...] = (a_ref[...].astype(F32) + b_ref[...].astype(F32)).astype(BF16)


def prep_kernel(share, at_ref, w_ref, *refs):
    *got_refs, m_ref, base_ref, wide_ref, flip_ref = refs
    pole = at_ref[0]
    block = m_ref.shape[1]
    for t in range(share):
        base = jnp.zeros((block, block), F32)
        for k, got_ref in enumerate(got_refs):
            inv = got_ref[t]
            base = base + w_ref[pole ^ (2 * k)] * inv.astype(F32)
            wide_ref[t, :, k * block:(k + 1) * block] = inv
            flip_ref[t, :, k * block:(k + 1) * block] = inv.T
        base_ref[t] = base
        m_ref[t] = (-base).astype(BF16)


def diag_kernel(share, at_ref, count_ref, w_ref, base_ref, wide_ref, flip_ref, *refs):
    *g_refs, out_ref = refs
    pole, col = at_ref[0], at_ref[1]
    block = base_ref.shape[1]
    half = wide_ref.shape[2] // block
    owned = share * half
    chunk = out_ref.shape[2]
    for t in range(share):
        count = count_ref[col * owned + (col ^ (share * (pole // 2) + t))]
        scale = 1.0 / (jnp.full((block, block), block, F32) * count.astype(F32))
        v = dot(g_refs[t // 2][t % 2], wide_ref[t])
        v = jnp.concatenate(
            [w_ref[pole ^ (2 * k)] * v[:, k * block:(k + 1) * block] for k in range(half)], axis=0
        )
        hi = v.astype(BF16)
        lo = (v - hi.astype(F32)).astype(BF16)
        flip = flip_ref[t]
        d = (base_ref[t] + (dot(flip, hi) + dot(flip, lo)) * scale).astype(BF16)
        for p in range(out_ref.shape[0]):
            out_ref[p, t] = d[p * chunk:(p + 1) * chunk]


def finish_kernel(share, at_ref, got_ref, out_ref):
    col = at_ref[1]
    for x in range(got_ref.shape[0] // 2):
        for t in range(share):
            d = got_ref[2 * x, t].astype(F32) + got_ref[2 * x + 1, t].astype(F32)
            out_ref[col ^ (share * x + t)] = d.astype(BF16)


def density_kernel(poles, share, at_ref, count_ref, moved_ref, *refs):
    *m_refs, out_ref = refs
    pole, col = at_ref[0], at_ref[1]
    owned, block = moved_ref.shape[0], moved_ref.shape[2]
    for k, m_ref in enumerate(m_refs):
        for t in range(share):
            i = col ^ (share * ((pole // 2) ^ k) + t)
            x = kept_rows(moved_ref.at[i], count_ref[col * owned + i], pole, poles, block)
            out_ref[i] = dot(x, m_ref[t]).astype(BF16)


def shards(panel, pivot_inverse, row_count, pole_weight):
    owned, rows, block = panel.shape
    poles = lax.axis_size("pole")
    cols = lax.axis_size("col")
    pole_at = lax.axis_index("pole")
    col_at = lax.axis_index("col")
    half = poles // 2
    share = owned // half
    chunk = block // poles
    at = jnp.stack([pole_at, col_at]).astype(jnp.int32)
    smem = pl.BlockSpec(memory_space=pltpu.SMEM)
    vmem = pl.BlockSpec(memory_space=pltpu.VMEM)
    shape = lambda *s: jax.ShapeDtypeStruct(s, BF16)

    def call(body, name, ins, outs, flops=0):
        moved_bytes = 2 * sum(o.size for o in outs) * 2
        return pl.pallas_call(
            body,
            in_specs=ins,
            out_specs=[vmem] * len(outs),
            out_shape=outs,
            compiler_params=pltpu.CompilerParams(vmem_limit_bytes=32 * 1024 * 1024),
            cost_estimate=pl.CostEstimate(flops=flops, bytes_accessed=moved_bytes, transcendentals=0),
            name=name,
        )

    def swap(x, k):
        return lax.ppermute(x, "pole", [(i, i ^ k) for i in range(poles)])

    moved = lax.all_to_all(panel, "col", 0, 0, tiled=True)

    sent = call(
        functools.partial(gram_kernel, poles, share), "gram",
        [smem, smem, vmem, vmem], [shape(share, block, block)] * poles,
        2 * owned * rows * block * block,
    )(at, row_count, panel, pivot_inverse[0])
    grams = [sent[0]] + [swap(sent[k], 2 * k) for k in range(1, half)]
    inverses = [sent[half]] + [swap(sent[half + k], 2 * k) for k in range(1, half)]

    keep, give = call(
        functools.partial(gsum_kernel, share), "gsum", [vmem] * half, [shape(share // 2, block, block)] * 2
    )(*grams)
    near = lax.ppermute(give, "col", [(c, c ^ 1) for c in range(cols)])
    ghalf = call(pair_kernel, "pair", [vmem] * 2, [shape(share // 2, 2, block, block)])(keep, near)[0]
    gfull = call(both_kernel, "gboth", [vmem] * 2, [shape(2, block, block)] * (share // 2))(ghalf, swap(ghalf, 1))

    def to_owner(g, f):
        return lax.ppermute(
            g, ("pole", "col"),
            [(p * cols + c, p * cols + (c ^ (share * (p // 2) + 2 * f))) for p in range(poles) for c in range(cols)],
        )

    gfull = [to_owner(g, f) for f, g in enumerate(gfull)]

    wide = shape(share, block, half * block)
    mhalf, base, wide, flip = call(
        functools.partial(prep_kernel, share), "prep", [smem, smem] + [vmem] * half,
        [shape(share, block, block), jax.ShapeDtypeStruct((share, block, block), F32), wide, wide],
    )(at, pole_weight, *inverses)
    mfull = call(add_kernel, "weights", [vmem] * 2, [shape(share, block, block)])(mhalf, swap(mhalf, 1))[0]
    mparts = [mfull] + [swap(mfull, 2 * k) for k in range(1, half)]

    part = call(
        functools.partial(diag_kernel, share), "diag",
        [smem, smem, smem, vmem, vmem, vmem] + [vmem] * (share // 2), [shape(poles, share, chunk, block)],
        6 * owned * block * block * block,
    )(at, row_count, pole_weight, base, wide, flip, *gfull)[0]
    part, moved = lax.optimization_barrier((part, moved))
    part = lax.all_to_all(part, "pole", 0, 0, tiled=True)
    diag = call(functools.partial(finish_kernel, share), "finish", [smem, vmem], [shape(owned, chunk, block)])(at, part)[0]

    density = call(
        functools.partial(density_kernel, poles, share), "density",
        [smem, smem, vmem] + [vmem] * half, [shape(owned, rows, block)],
        2 * owned * rows * block * block,
    )(at, row_count, moved, *mparts)[0]
    return density, diag


def solution(mesh):
    placed = (P("col", "pole", None), P("pole", "col", None, None), P(), P())
    return jax.shard_map(
        shards,
        mesh=mesh,
        in_specs=placed,
        out_specs=(P("col", "pole", None), P("col", "pole", None)),
        check_vma=False,
    )
```

```python
import functools

import jax
import jax.numpy as jnp
from jax import lax
from jax.experimental import pallas as pl
from jax.experimental.pallas import tpu as pltpu
from jax.sharding import PartitionSpec as P

F32 = jnp.float32
BF16 = jnp.bfloat16


def dot(a, b):
    return lax.dot_general(a, b, (((1,), (0,)), ((), ())), preferred_element_type=F32)


def dot_t(a, b):
    return lax.dot_general(a, b, (((0,), (0,)), ((), ())), preferred_element_type=F32)


def kept_rows(source, count, pole, poles, block):
    zero = jnp.zeros((block, block), BF16)
    rows_local = source.shape[0] // block
    return jnp.concatenate(
        [
            lax.select(k * poles + pole < count, source[pl.ds(k * block, block), :], zero)
            for k in range(rows_local)
        ],
        axis=0,
    )


def gram_kernel(poles, share, at_ref, count_ref, panel_ref, inv_ref, *out_refs):
    pole, col = at_ref[0], at_ref[1]
    owned, block = inv_ref.shape[0], inv_ref.shape[1]
    half = len(out_refs) // 2
    for k in range(half):
        for t in range(share):
            i = col ^ (share * ((pole // 2) ^ k) + t)
            x = kept_rows(panel_ref.at[i], count_ref[i * owned + col], pole, poles, block)
            out_refs[k][t] = dot_t(x, x).astype(BF16)
            out_refs[half + k][t] = inv_ref[i]


def gsum_kernel(share, *refs):
    *got_refs, keep_ref, give_ref = refs
    for t in range(share):
        g = sum(got_ref[t].astype(F32) for got_ref in got_refs).astype(BF16)
        (give_ref if t % 2 else keep_ref)[t // 2] = g


def pair_kernel(a_ref, b_ref, out_ref):
    out_ref[:, 0] = a_ref[...]
    out_ref[:, 1] = b_ref[...]


def both_kernel(a_ref, b_ref, *out_refs):
    for t, out_ref in enumerate(out_refs):
        out_ref[...] = (a_ref[t].astype(F32) + b_ref[t].astype(F32)).astype(BF16)


def add_kernel(a_ref, b_ref, out_ref):
    out_ref[...] = (a_ref[...].astype(F32) + b_ref[...].astype(F32)).astype(BF16)


def prep_kernel(share, at_ref, w_ref, count_ref, *refs):
    *got_refs, m_ref, base_ref, gain_ref, wide_ref, flip_ref = refs
    pole, col = at_ref[0], at_ref[1]
    block = m_ref.shape[1]
    owned = share * len(got_refs)
    for t in range(share):
        count = count_ref[col * owned + (col ^ (share * (pole // 2) + t))]
        scale = 1.0 / (jnp.full((1, block), block, F32) * count.astype(F32))
        base = jnp.zeros((block, block), F32)
        for k, got_ref in enumerate(got_refs):
            inv = got_ref[t]
            w = w_ref[pole ^ (2 * k)]
            base = base + w * inv.astype(F32)
            gain_ref[t, :, k * block:(k + 1) * block] = w * scale
            wide_ref[t, :, k * block:(k + 1) * block] = inv
            flip_ref[t, :, k * block:(k + 1) * block] = inv.T
        base_ref[t] = base
        m_ref[t] = (-base).astype(BF16)


def diag_kernel(share, base_ref, gain_ref, wide_ref, flip_ref, *refs):
    *g_refs, out_ref = refs
    block = base_ref.shape[1]
    half = wide_ref.shape[2] // block
    chunk = out_ref.shape[2]
    for t in range(share):
        g = g_refs[t // 2][t % 2]
        v = dot(g, wide_ref[t]) * gain_ref[t]
        v = jnp.concatenate([v[:, k * block:(k + 1) * block] for k in range(half)], axis=0)
        hi = v.astype(BF16)
        lo = (v - hi.astype(F32)).astype(BF16)
        flip = flip_ref[t]
        d = (base_ref[t] + dot(flip, hi) + dot(flip, lo)).astype(BF16)
        for p in range(out_ref.shape[0]):
            out_ref[p, t] = d[p * chunk:(p + 1) * chunk]


def finish_kernel(share, got_ref, out_ref):
    col = lax.axis_index("col")
    for x in range(got_ref.shape[0] // 2):
        for t in range(share):
            d = got_ref[2 * x, t].astype(F32) + got_ref[2 * x + 1, t].astype(F32)
            out_ref[col ^ (share * x + t)] = d.astype(BF16)


def density_kernel(poles, share, at_ref, count_ref, moved_ref, *refs):
    *m_refs, out_ref = refs
    pole, col = at_ref[0], at_ref[1]
    owned, block = moved_ref.shape[0], moved_ref.shape[2]
    for k, m_ref in enumerate(m_refs):
        for t in range(share):
            i = col ^ (share * ((pole // 2) ^ k) + t)
            x = kept_rows(moved_ref.at[i], count_ref[col * owned + i], pole, poles, block)
            out_ref[i] = dot(x, m_ref[t]).astype(BF16)


def shards(panel, pivot_inverse, row_count, pole_weight):
    owned, rows, block = panel.shape
    poles = lax.axis_size("pole")
    cols = lax.axis_size("col")
    pole_at = lax.axis_index("pole")
    col_at = lax.axis_index("col")
    half = poles // 2
    share = owned // half
    chunk = block // poles
    at = jnp.stack([pole_at, col_at]).astype(jnp.int32)
    smem = pl.BlockSpec(memory_space=pltpu.SMEM)
    vmem = pl.BlockSpec(memory_space=pltpu.VMEM)
    shape = lambda *s: jax.ShapeDtypeStruct(s, BF16)

    def call(body, name, ins, outs, flops=0):
        moved_bytes = 2 * sum(o.size for o in outs) * 2
        return pl.pallas_call(
            body,
            in_specs=ins,
            out_specs=[vmem] * len(outs),
            out_shape=outs,
            compiler_params=pltpu.CompilerParams(vmem_limit_bytes=32 * 1024 * 1024),
            cost_estimate=pl.CostEstimate(flops=flops, bytes_accessed=moved_bytes, transcendentals=0),
            name=name,
        )

    def swap(x, k):
        return lax.ppermute(x, "pole", [(i, i ^ k) for i in range(poles)])

    moved = lax.all_to_all(panel, "col", 0, 0, tiled=True)

    sent = call(
        functools.partial(gram_kernel, poles, share), "gram",
        [smem, smem, vmem, vmem], [shape(share, block, block)] * poles,
        2 * owned * rows * block * block,
    )(at, row_count, panel, pivot_inverse[0])
    grams = [sent[0]] + [swap(sent[k], 2 * k) for k in range(1, half)]
    inverses = [sent[half]] + [swap(sent[half + k], 2 * k) for k in range(1, half)]

    keep, give = call(
        functools.partial(gsum_kernel, share), "gsum", [vmem] * half, [shape(share // 2, block, block)] * 2
    )(*grams)
    near = lax.ppermute(give, "col", [(c, c ^ 1) for c in range(cols)])
    ghalf = call(pair_kernel, "pair", [vmem] * 2, [shape(share // 2, 2, block, block)])(keep, near)[0]

    gfull = call(
        both_kernel, "gboth", [vmem] * 2, [shape(2, block, block)] * (share // 2)
    )(ghalf, swap(ghalf, 1))

    def to_owner(g, f):
        return lax.ppermute(
            g, ("pole", "col"),
            [(p * cols + c, p * cols + (c ^ (share * (p // 2) + 2 * f))) for p in range(poles) for c in range(cols)],
        )

    gparts = [to_owner(g, f) for f, g in enumerate(gfull)]

    wide = shape(share, block, half * block)
    mhalf, base, gain, wide, flip = call(
        functools.partial(prep_kernel, share), "prep", [smem] * 3 + [vmem] * half,
        [shape(share, block, block), jax.ShapeDtypeStruct((share, block, block), F32), jax.ShapeDtypeStruct((share, 1, half * block), F32), wide, wide],
    )(at, pole_weight, row_count, *inverses)
    mfull = call(add_kernel, "weights", [vmem] * 2, [shape(share, block, block)])(mhalf, swap(mhalf, 1))[0]
    mparts = [mfull] + [swap(mfull, 2 * k) for k in range(1, half)]

    part = call(
        functools.partial(diag_kernel, share), "diag",
        [vmem] * (4 + share // 2), [shape(poles, share, chunk, block)],
        6 * owned * block * block * block,
    )(base, gain, wide, flip, *gparts)[0]
    part, moved = lax.optimization_barrier((part, moved))
    part = lax.all_to_all(part, "pole", 0, 0, tiled=True)
    diag = call(functools.partial(finish_kernel, share), "finish", [vmem], [shape(owned, chunk, block)])(part)[0]

    density = call(
        functools.partial(density_kernel, poles, share), "density",
        [smem, smem, vmem] + [vmem] * half, [shape(owned, rows, block)],
        2 * owned * rows * block * block,
    )(at, row_count, moved, *mparts)[0]
    return density, diag


def solution(mesh):
    placed = (P("col", "pole", None), P("pole", "col", None, None), P(), P())
    return jax.shard_map(
        shards,
        mesh=mesh,
        in_specs=placed,
        out_specs=(P("col", "pole", None), P("col", "pole", None)),
        check_vma=False,
    )
```

```python
import functools

import jax
import jax.numpy as jnp
from jax import lax
from jax.experimental import pallas as pl
from jax.experimental.pallas import tpu as pltpu
from jax.sharding import PartitionSpec as P

F32 = jnp.float32
BF16 = jnp.bfloat16


def dot(a, b):
    return lax.dot_general(a, b, (((1,), (0,)), ((), ())), preferred_element_type=F32)


def dot_t(a, b):
    return lax.dot_general(a, b, (((0,), (0,)), ((), ())), preferred_element_type=F32)


def kept_rows(source, count, pole, poles, block):
    zero = jnp.zeros((block, block), BF16)
    rows_local = source.shape[0] // block
    return jnp.concatenate(
        [
            lax.select(k * poles + pole < count, source[pl.ds(k * block, block), :], zero)
            for k in range(rows_local)
        ],
        axis=0,
    )


def gram_kernel(poles, share, at_ref, count_ref, panel_ref, inv_ref, *out_refs):
    pole, col = at_ref[0], at_ref[1]
    owned, block = inv_ref.shape[0], inv_ref.shape[1]
    half = len(out_refs) // 2
    for k in range(half):
        for t in range(share):
            i = col ^ (share * ((pole // 2) ^ k) + t)
            x = kept_rows(panel_ref.at[i], count_ref[i * owned + col], pole, poles, block)
            out_refs[k][t] = dot_t(x, x).astype(BF16)
            out_refs[half + k][t] = inv_ref[i]


def gsum_kernel(share, *refs):
    *got_refs, keep_ref, give_ref = refs
    for t in range(share):
        g = sum(got_ref[t].astype(F32) for got_ref in got_refs).astype(BF16)
        (give_ref if t % 2 else keep_ref)[t // 2] = g


def pair_kernel(a_ref, b_ref, *out_refs):
    for f, out_ref in enumerate(out_refs):
        out_ref[0] = a_ref[f]
        out_ref[1] = b_ref[f]


def gown_kernel(a0_ref, a1_ref, b0_ref, b1_ref, out_ref):
    for f, (x_ref, y_ref) in enumerate(((a0_ref, a1_ref), (b0_ref, b1_ref))):
        out_ref[f] = (x_ref[...].astype(F32) + y_ref[...].astype(F32)).astype(BF16)


def add_kernel(a_ref, b_ref, out_ref):
    out_ref[...] = (a_ref[...].astype(F32) + b_ref[...].astype(F32)).astype(BF16)


def prep_kernel(share, at_ref, w_ref, count_ref, *refs):
    *got_refs, m_ref, base_ref, gain_ref, wide_ref, flip_ref = refs
    pole, col = at_ref[0], at_ref[1]
    block = m_ref.shape[1]
    owned = share * len(got_refs)
    for t in range(share):
        count = count_ref[col * owned + (col ^ (share * (pole // 2) + t))]
        scale = 1.0 / (jnp.full((1, block), block, F32) * count.astype(F32))
        base = jnp.zeros((block, block), F32)
        for k, got_ref in enumerate(got_refs):
            inv = got_ref[t]
            w = w_ref[pole ^ (2 * k)]
            base = base + w * inv.astype(F32)
            gain_ref[t, :, k * block:(k + 1) * block] = w * scale
            wide_ref[t, :, k * block:(k + 1) * block] = inv
            flip_ref[t, :, k * block:(k + 1) * block] = inv.T
        base_ref[t] = base
        m_ref[t] = (-base).astype(BF16)


def diag_kernel(share, base_ref, gain_ref, wide_ref, flip_ref, *refs):
    g_ref, out_ref = refs
    block = base_ref.shape[1]
    half = wide_ref.shape[2] // block
    chunk = out_ref.shape[2]
    for t in range(share):
        g = g_ref[t // 2, t % 2]
        v = dot(g, wide_ref[t]) * gain_ref[t]
        v = jnp.concatenate([v[:, k * block:(k + 1) * block] for k in range(half)], axis=0)
        hi = v.astype(BF16)
        lo = (v - hi.astype(F32)).astype(BF16)
        flip = flip_ref[t]
        d = (base_ref[t] + dot(flip, hi) + dot(flip, lo)).astype(BF16)
        for p in range(out_ref.shape[0]):
            out_ref[p, t] = d[p * chunk:(p + 1) * chunk]


def finish_kernel(share, got_ref, out_ref):
    col = lax.axis_index("col")
    for x in range(got_ref.shape[0] // 2):
        for t in range(share):
            d = got_ref[2 * x, t].astype(F32) + got_ref[2 * x + 1, t].astype(F32)
            out_ref[col ^ (share * x + t)] = d.astype(BF16)


def density_kernel(poles, share, at_ref, count_ref, moved_ref, *refs):
    *m_refs, out_ref = refs
    pole, col = at_ref[0], at_ref[1]
    owned, block = moved_ref.shape[0], moved_ref.shape[2]
    for k, m_ref in enumerate(m_refs):
        for t in range(share):
            i = col ^ (share * ((pole // 2) ^ k) + t)
            x = kept_rows(moved_ref.at[i], count_ref[col * owned + i], pole, poles, block)
            out_ref[i] = dot(x, m_ref[t]).astype(BF16)


def shards(panel, pivot_inverse, row_count, pole_weight):
    owned, rows, block = panel.shape
    poles = lax.axis_size("pole")
    cols = lax.axis_size("col")
    pole_at = lax.axis_index("pole")
    col_at = lax.axis_index("col")
    half = poles // 2
    share = owned // half
    chunk = block // poles
    at = jnp.stack([pole_at, col_at]).astype(jnp.int32)
    smem = pl.BlockSpec(memory_space=pltpu.SMEM)
    vmem = pl.BlockSpec(memory_space=pltpu.VMEM)
    shape = lambda *s: jax.ShapeDtypeStruct(s, BF16)

    def call(body, name, ins, outs, flops=0):
        moved_bytes = 2 * sum(o.size for o in outs) * 2
        return pl.pallas_call(
            body,
            in_specs=ins,
            out_specs=[vmem] * len(outs),
            out_shape=outs,
            compiler_params=pltpu.CompilerParams(vmem_limit_bytes=32 * 1024 * 1024),
            cost_estimate=pl.CostEstimate(flops=flops, bytes_accessed=moved_bytes, transcendentals=0),
            name=name,
        )

    def swap(x, k):
        return lax.ppermute(x, "pole", [(i, i ^ k) for i in range(poles)])

    moved = lax.all_to_all(panel, "col", 0, 0, tiled=True)

    sent = call(
        functools.partial(gram_kernel, poles, share), "gram",
        [smem, smem, vmem, vmem], [shape(share, block, block)] * poles,
        2 * owned * rows * block * block,
    )(at, row_count, panel, pivot_inverse[0])
    grams = [sent[0]] + [swap(sent[k], 2 * k) for k in range(1, half)]
    inverses = [sent[half]] + [swap(sent[half + k], 2 * k) for k in range(1, half)]

    keep, give = call(
        functools.partial(gsum_kernel, share), "gsum", [vmem] * half, [shape(share // 2, block, block)] * 2
    )(*grams)
    near = lax.ppermute(give, "col", [(c, c ^ 1) for c in range(cols)])
    here, side = call(pair_kernel, "pair", [vmem] * 2, [shape(2, block, block)] * 2)(keep, near)

    def shift(x, z, flip):
        pairs = [(p * cols + c, (p ^ z) * cols + (c ^ flip(p))) for p in range(poles) for c in range(cols)]
        return lax.ppermute(x, ("pole", "col"), pairs)

    line = lambda p: 2
    gfull = call(gown_kernel, "gown", [vmem] * 4, [shape(2, 2, block, block)])(
        here, swap(here, 1), shift(side, 0, line), shift(side, 1, line)
    )[0]
    gfull = shift(gfull, 0, lambda p: share * (p // 2))

    wide = shape(share, block, half * block)
    mhalf, base, gain, wide, flip = call(
        functools.partial(prep_kernel, share), "prep", [smem] * 3 + [vmem] * half,
        [shape(share, block, block), jax.ShapeDtypeStruct((share, block, block), F32), jax.ShapeDtypeStruct((share, 1, half * block), F32), wide, wide],
    )(at, pole_weight, row_count, *inverses)
    mfull = call(add_kernel, "weights", [vmem] * 2, [shape(share, block, block)])(mhalf, swap(mhalf, 1))[0]
    mparts = [mfull] + [swap(mfull, 2 * k) for k in range(1, half)]

    part = call(
        functools.partial(diag_kernel, share), "diag",
        [vmem] * 5, [shape(poles, share, chunk, block)],
        6 * owned * block * block * block,
    )(base, gain, wide, flip, gfull)[0]
    part, moved = lax.optimization_barrier((part, moved))
    part = lax.all_to_all(part, "pole", 0, 0, tiled=True)
    diag = call(functools.partial(finish_kernel, share), "finish", [vmem], [shape(owned, chunk, block)])(part)[0]

    density = call(
        functools.partial(density_kernel, poles, share), "density",
        [smem, smem, vmem] + [vmem] * half, [shape(owned, rows, block)],
        2 * owned * rows * block * block,
    )(at, row_count, moved, *mparts)[0]
    return density, diag


def solution(mesh):
    placed = (P("col", "pole", None), P("pole", "col", None, None), P(), P())
    return jax.shard_map(
        shards,
        mesh=mesh,
        in_specs=placed,
        out_specs=(P("col", "pole", None), P("col", "pole", None)),
        check_vma=False,
    )
```

```python
import functools

import jax
import jax.numpy as jnp
from jax import lax
from jax.experimental import pallas as pl
from jax.experimental.pallas import tpu as pltpu
from jax.sharding import PartitionSpec as P

F32 = jnp.float32
BF16 = jnp.bfloat16


def dot(a, b):
    return lax.dot_general(a, b, (((1,), (0,)), ((), ())), preferred_element_type=F32)


def dot_t(a, b):
    return lax.dot_general(a, b, (((0,), (0,)), ((), ())), preferred_element_type=F32)


def slot(share, x, t):
    return 2 * x + 2 * share * (t // 2) + t % 2


def kept_rows(source, count, pole, poles, block):
    zero = jnp.zeros((block, block), BF16)
    rows_local = source.shape[0] // block
    return jnp.concatenate(
        [
            lax.select(k * poles + pole < count, source[pl.ds(k * block, block), :], zero)
            for k in range(rows_local)
        ],
        axis=0,
    )


def gram_kernel(poles, share, at_ref, count_ref, panel_ref, *out_refs):
    pole, col = at_ref[0], at_ref[1]
    owned, block = panel_ref.shape[0], panel_ref.shape[2]
    for k, out_ref in enumerate(out_refs):
        for t in range(share):
            i = col ^ slot(share, (pole // 2) ^ k, t)
            x = kept_rows(panel_ref.at[i], count_ref[i * owned + col], pole, poles, block)
            out_ref[t] = dot_t(x, x).astype(BF16)


def turn_kernel(share, inv_ref, *out_refs):
    pole, col = lax.axis_index("pole"), lax.axis_index("col")
    for k, out_ref in enumerate(out_refs):
        for t in range(share):
            out_ref[t] = inv_ref[col ^ slot(share, (pole // 2) ^ k, t)]


def gsum_kernel(share, *refs):
    *got_refs, keep_ref, give_ref = refs
    for t in range(share):
        g = sum(got_ref[t].astype(F32) for got_ref in got_refs).astype(BF16)
        (give_ref if t % 2 else keep_ref)[t // 2] = g


def pair_kernel(a_ref, b_ref, *out_refs):
    for f, out_ref in enumerate(out_refs):
        out_ref[0] = a_ref[f]
        out_ref[1] = b_ref[f]


def gown_kernel(a0_ref, a1_ref, b0_ref, b1_ref, out_ref):
    for f, (x_ref, y_ref) in enumerate(((a0_ref, a1_ref), (b0_ref, b1_ref))):
        out_ref[f] = (x_ref[...].astype(F32) + y_ref[...].astype(F32)).astype(BF16)


def add_kernel(a_ref, b_ref, out_ref):
    out_ref[...] = (a_ref[...].astype(F32) + b_ref[...].astype(F32)).astype(BF16)


def prep_kernel(share, at_ref, w_ref, count_ref, *refs):
    *got_refs, m_ref, base_ref, gain_ref, wide_ref, flip_ref = refs
    pole, col = at_ref[0], at_ref[1]
    block = m_ref.shape[1]
    owned = share * len(got_refs)
    for t in range(share):
        count = count_ref[col * owned + (col ^ slot(share, pole // 2, t))]
        scale = 1.0 / (jnp.full((1, block), block, F32) * count.astype(F32))
        base = jnp.zeros((block, block), F32)
        for k, got_ref in enumerate(got_refs):
            inv = got_ref[t]
            w = w_ref[pole ^ (2 * k)]
            base = base + w * inv.astype(F32)
            gain_ref[t, :, k * block:(k + 1) * block] = w * scale
            wide_ref[t, :, k * block:(k + 1) * block] = inv
            flip_ref[t, :, k * block:(k + 1) * block] = inv.T
        base_ref[t] = base
        m_ref[t] = (-base).astype(BF16)


def diag_kernel(share, base_ref, gain_ref, wide_ref, flip_ref, *refs):
    g_ref, out_ref = refs
    block = base_ref.shape[1]
    half = wide_ref.shape[2] // block
    chunk = out_ref.shape[2]
    for t in range(share):
        g = g_ref[t // 2, t % 2]
        v = dot(g, wide_ref[t]) * gain_ref[t]
        v = jnp.concatenate([v[:, k * block:(k + 1) * block] for k in range(half)], axis=0)
        hi = v.astype(BF16)
        lo = (v - hi.astype(F32)).astype(BF16)
        flip = flip_ref[t]
        d = (base_ref[t] + dot(flip, hi) + dot(flip, lo)).astype(BF16)
        for p in range(out_ref.shape[0]):
            out_ref[p, t] = d[p * chunk:(p + 1) * chunk]


def finish_kernel(share, got_ref, out_ref):
    col = lax.axis_index("col")
    for x in range(got_ref.shape[0] // 2):
        for t in range(share):
            d = got_ref[2 * x, t].astype(F32) + got_ref[2 * x + 1, t].astype(F32)
            out_ref[col ^ slot(share, x, t)] = d.astype(BF16)


def density_kernel(poles, share, at_ref, count_ref, moved_ref, *refs):
    *m_refs, out_ref = refs
    pole, col = at_ref[0], at_ref[1]
    owned, block = moved_ref.shape[0], moved_ref.shape[2]
    for k, m_ref in enumerate(m_refs):
        for t in range(share):
            i = col ^ slot(share, (pole // 2) ^ k, t)
            x = kept_rows(moved_ref.at[i], count_ref[col * owned + i], pole, poles, block)
            out_ref[i] = dot(x, m_ref[t]).astype(BF16)


def shards(panel, pivot_inverse, row_count, pole_weight):
    owned, rows, block = panel.shape
    poles = lax.axis_size("pole")
    cols = lax.axis_size("col")
    pole_at = lax.axis_index("pole")
    col_at = lax.axis_index("col")
    half = poles // 2
    share = owned // half
    chunk = block // poles
    at = jnp.stack([pole_at, col_at]).astype(jnp.int32)
    smem = pl.BlockSpec(memory_space=pltpu.SMEM)
    vmem = pl.BlockSpec(memory_space=pltpu.VMEM)
    shape = lambda *s: jax.ShapeDtypeStruct(s, BF16)

    def call(body, name, ins, outs, flops=0):
        moved_bytes = 2 * sum(o.size for o in outs) * 2
        return pl.pallas_call(
            body,
            in_specs=ins,
            out_specs=[vmem] * len(outs),
            out_shape=outs,
            compiler_params=pltpu.CompilerParams(vmem_limit_bytes=32 * 1024 * 1024),
            cost_estimate=pl.CostEstimate(flops=flops, bytes_accessed=moved_bytes, transcendentals=0),
            name=name,
        )

    def swap(x, k):
        return lax.ppermute(x, "pole", [(i, i ^ k) for i in range(poles)])

    moved = lax.all_to_all(panel, "col", 0, 0, tiled=True)

    turned = call(
        functools.partial(turn_kernel, share), "turn", [vmem], [shape(share, block, block)] * half
    )(pivot_inverse[0])
    sent = call(
        functools.partial(gram_kernel, poles, share), "gram",
        [smem, smem, vmem], [shape(share, block, block)] * half,
        2 * owned * rows * block * block,
    )(at, row_count, panel)
    grams = [sent[0]] + [swap(sent[k], 2 * k) for k in range(1, half)]
    inverses = [turned[0]] + [swap(turned[k], 2 * k) for k in range(1, half)]

    keep, give = call(
        functools.partial(gsum_kernel, share), "gsum", [vmem] * half, [shape(share // 2, block, block)] * 2
    )(*grams)
    near = lax.ppermute(give, "col", [(c, c ^ 1) for c in range(cols)])
    here, side = call(pair_kernel, "pair", [vmem] * 2, [shape(2, block, block)] * 2)(keep, near)

    def shift(x, z, flip):
        pairs = [(p * cols + c, (p ^ z) * cols + (c ^ flip(p))) for p in range(poles) for c in range(cols)]
        return lax.ppermute(x, ("pole", "col"), pairs)

    over = lambda p: 2 * share
    gfull = call(gown_kernel, "gown", [vmem] * 4, [shape(2, 2, block, block)])(
        here, swap(here, 1), shift(side, 0, over), shift(side, 1, over)
    )[0]
    gfull = shift(gfull, 0, lambda p: 2 * (p // 2))

    wide = shape(share, block, half * block)
    mhalf, base, gain, wide, flip = call(
        functools.partial(prep_kernel, share), "prep", [smem] * 3 + [vmem] * half,
        [shape(share, block, block), jax.ShapeDtypeStruct((share, block, block), F32), jax.ShapeDtypeStruct((share, 1, half * block), F32), wide, wide],
    )(at, pole_weight, row_count, *inverses)
    mfull = call(add_kernel, "weights", [vmem] * 2, [shape(share, block, block)])(mhalf, swap(mhalf, 1))[0]
    mparts = [mfull] + [swap(mfull, 2 * k) for k in range(1, half)]

    part = call(
        functools.partial(diag_kernel, share), "diag",
        [vmem] * 5, [shape(poles, share, chunk, block)],
        6 * owned * block * block * block,
    )(base, gain, wide, flip, gfull)[0]
    part, moved = lax.optimization_barrier((part, moved))
    part = lax.all_to_all(part, "pole", 0, 0, tiled=True)
    diag = call(functools.partial(finish_kernel, share), "finish", [vmem], [shape(owned, chunk, block)])(part)[0]

    density = call(
        functools.partial(density_kernel, poles, share), "density",
        [smem, smem, vmem] + [vmem] * half, [shape(owned, rows, block)],
        2 * owned * rows * block * block,
    )(at, row_count, moved, *mparts)[0]
    return density, diag


def solution(mesh):
    placed = (P("col", "pole", None), P("pole", "col", None, None), P(), P())
    return jax.shard_map(
        shards,
        mesh=mesh,
        in_specs=placed,
        out_specs=(P("col", "pole", None), P("col", "pole", None)),
        check_vma=False,
    )
```

```python
import functools

import jax
import jax.numpy as jnp
from jax import lax
from jax.experimental import pallas as pl
from jax.experimental.pallas import tpu as pltpu
from jax.sharding import PartitionSpec as P

F32 = jnp.float32
BF16 = jnp.bfloat16


def dot(a, b):
    return lax.dot_general(a, b, (((1,), (0,)), ((), ())), preferred_element_type=F32)


def dot_t(a, b):
    return lax.dot_general(a, b, (((0,), (0,)), ((), ())), preferred_element_type=F32)


def slot(share, x, t):
    return 2 * x + 2 * share * (t // 2) + t % 2


def kept_rows(source, count, pole, poles, block):
    zero = jnp.zeros((block, block), BF16)
    rows_local = source.shape[0] // block
    return jnp.concatenate(
        [
            lax.select(k * poles + pole < count, source[pl.ds(k * block, block), :], zero)
            for k in range(rows_local)
        ],
        axis=0,
    )


def gram_kernel(poles, share, at_ref, count_ref, panel_ref, *out_refs):
    pole, col = at_ref[0], at_ref[1]
    owned, block = panel_ref.shape[0], panel_ref.shape[2]
    for k, out_ref in enumerate(out_refs):
        for t in range(share):
            i = col ^ slot(share, (pole // 2) ^ k, t)
            x = kept_rows(panel_ref.at[i], count_ref[i * owned + col], pole, poles, block)
            out_ref[t] = dot_t(x, x).astype(BF16)


def turn_kernel(share, inv_ref, *out_refs):
    pole, col = lax.axis_index("pole"), lax.axis_index("col")
    for k, out_ref in enumerate(out_refs):
        for t in range(share):
            out_ref[t] = inv_ref[col ^ slot(share, (pole // 2) ^ k, t)]


def gsum_kernel(share, *refs):
    *got_refs, keep_ref, give_ref = refs
    for t in range(share):
        g = sum(got_ref[t].astype(F32) for got_ref in got_refs).astype(BF16)
        (give_ref if t % 2 else keep_ref)[t // 2] = g


def pair_kernel(a_ref, b_ref, *out_refs):
    for f, out_ref in enumerate(out_refs):
        out_ref[0] = a_ref[f]
        out_ref[1] = b_ref[f]


def gown_kernel(b0_ref, b1_ref, a0_ref, a1_ref, out_ref):
    for f, (x_ref, y_ref) in enumerate(((a0_ref, a1_ref), (b0_ref, b1_ref))):
        out_ref[f] = (x_ref[...].astype(F32) + y_ref[...].astype(F32)).astype(BF16)


def add_kernel(a_ref, b_ref, out_ref):
    out_ref[...] = (a_ref[...].astype(F32) + b_ref[...].astype(F32)).astype(BF16)


def prep_kernel(share, at_ref, w_ref, count_ref, *refs):
    *got_refs, m_ref, base_ref, gain_ref, wide_ref, flip_ref = refs
    pole, col = at_ref[0], at_ref[1]
    block = m_ref.shape[1]
    owned = share * len(got_refs)
    for t in range(share):
        count = count_ref[col * owned + (col ^ slot(share, pole // 2, t))]
        scale = 1.0 / (jnp.full((1, block), block, F32) * count.astype(F32))
        base = jnp.zeros((block, block), F32)
        for k, got_ref in enumerate(got_refs):
            inv = got_ref[t]
            w = w_ref[pole ^ (2 * k)]
            base = base + w * inv.astype(F32)
            gain_ref[t, :, k * block:(k + 1) * block] = w * scale
            wide_ref[t, :, k * block:(k + 1) * block] = inv
            flip_ref[t, :, k * block:(k + 1) * block] = inv.T
        base_ref[t] = base
        m_ref[t] = (-base).astype(BF16)


def diag_kernel(share, base_ref, gain_ref, wide_ref, flip_ref, *refs):
    g_ref, out_ref = refs
    block = base_ref.shape[1]
    half = wide_ref.shape[2] // block
    chunk = out_ref.shape[2]
    for t in range(share):
        g = g_ref[t // 2, t % 2]
        v = dot(g, wide_ref[t]) * gain_ref[t]
        v = jnp.concatenate([v[:, k * block:(k + 1) * block] for k in range(half)], axis=0)
        hi = v.astype(BF16)
        lo = (v - hi.astype(F32)).astype(BF16)
        flip = flip_ref[t]
        d = (base_ref[t] + dot(flip, hi) + dot(flip, lo)).astype(BF16)
        for p in range(out_ref.shape[0]):
            out_ref[p, t] = d[p * chunk:(p + 1) * chunk]


def finish_kernel(share, got_ref, out_ref):
    col = lax.axis_index("col")
    for x in range(got_ref.shape[0] // 2):
        for t in range(share):
            d = got_ref[2 * x, t].astype(F32) + got_ref[2 * x + 1, t].astype(F32)
            out_ref[col ^ slot(share, x, t)] = d.astype(BF16)


def density_kernel(poles, share, at_ref, count_ref, moved_ref, *refs):
    *m_refs, out_ref = refs
    pole, col = at_ref[0], at_ref[1]
    owned, block = moved_ref.shape[0], moved_ref.shape[2]
    for k, m_ref in enumerate(m_refs):
        for t in range(share):
            i = col ^ slot(share, (pole // 2) ^ k, t)
            x = kept_rows(moved_ref.at[i], count_ref[col * owned + i], pole, poles, block)
            out_ref[i] = dot(x, m_ref[t]).astype(BF16)


def shards(panel, pivot_inverse, row_count, pole_weight):
    owned, rows, block = panel.shape
    poles = lax.axis_size("pole")
    cols = lax.axis_size("col")
    pole_at = lax.axis_index("pole")
    col_at = lax.axis_index("col")
    half = poles // 2
    share = owned // half
    chunk = block // poles
    at = jnp.stack([pole_at, col_at]).astype(jnp.int32)
    smem = pl.BlockSpec(memory_space=pltpu.SMEM)
    vmem = pl.BlockSpec(memory_space=pltpu.VMEM)
    shape = lambda *s: jax.ShapeDtypeStruct(s, BF16)

    def call(body, name, ins, outs, flops=0):
        moved_bytes = 2 * sum(o.size for o in outs) * 2
        return pl.pallas_call(
            body,
            in_specs=ins,
            out_specs=[vmem] * len(outs),
            out_shape=outs,
            compiler_params=pltpu.CompilerParams(vmem_limit_bytes=32 * 1024 * 1024),
            cost_estimate=pl.CostEstimate(flops=flops, bytes_accessed=moved_bytes, transcendentals=0),
            name=name,
        )

    def swap(x, k):
        return lax.ppermute(x, "pole", [(i, i ^ k) for i in range(poles)])

    moved = lax.all_to_all(panel, "col", 0, 0, tiled=True)

    turned = call(
        functools.partial(turn_kernel, share), "turn", [vmem], [shape(share, block, block)] * half
    )(pivot_inverse[0])
    sent = call(
        functools.partial(gram_kernel, poles, share), "gram",
        [smem, smem, vmem], [shape(share, block, block)] * half,
        2 * owned * rows * block * block,
    )(at, row_count, panel)
    grams = [sent[0]] + [swap(sent[k], 2 * k) for k in range(1, half)]
    inverses = [turned[0]] + [swap(turned[k], 2 * k) for k in range(1, half)]

    keep, give = call(
        functools.partial(gsum_kernel, share), "gsum", [vmem] * half, [shape(share // 2, block, block)] * 2
    )(*grams)
    near = lax.ppermute(give, "col", [(c, c ^ 1) for c in range(cols)])
    here, side = call(pair_kernel, "pair", [vmem] * 2, [shape(2, block, block)] * 2)(keep, near)

    def shift(x, z, flip):
        pairs = [(p * cols + c, (p ^ z) * cols + (c ^ flip(p))) for p in range(poles) for c in range(cols)]
        return lax.ppermute(x, ("pole", "col"), pairs)

    over = lambda p: 2 * share
    gfull = call(gown_kernel, "gown", [vmem] * 4, [shape(2, 2, block, block)])(
        shift(side, 1, over), shift(side, 0, over), here, swap(here, 1)
    )[0]
    gfull = shift(gfull, 0, lambda p: 2 * (p // 2))

    wide = shape(share, block, half * block)
    mhalf, base, gain, wide, flip = call(
        functools.partial(prep_kernel, share), "prep", [smem] * 3 + [vmem] * half,
        [shape(share, block, block), jax.ShapeDtypeStruct((share, block, block), F32), jax.ShapeDtypeStruct((share, 1, half * block), F32), wide, wide],
    )(at, pole_weight, row_count, *inverses)
    mfull = call(add_kernel, "weights", [vmem] * 2, [shape(share, block, block)])(mhalf, swap(mhalf, 1))[0]
    mparts = [mfull] + [swap(mfull, 2 * k) for k in range(1, half)]

    part = call(
        functools.partial(diag_kernel, share), "diag",
        [vmem] * 5, [shape(poles, share, chunk, block)],
        6 * owned * block * block * block,
    )(base, gain, wide, flip, gfull)[0]
    part, moved = lax.optimization_barrier((part, moved))
    part = lax.all_to_all(part, "pole", 0, 0, tiled=True)
    diag = call(functools.partial(finish_kernel, share), "finish", [vmem], [shape(owned, chunk, block)])(part)[0]

    density = call(
        functools.partial(density_kernel, poles, share), "density",
        [smem, smem, vmem] + [vmem] * half, [shape(owned, rows, block)],
        2 * owned * rows * block * block,
    )(at, row_count, moved, *mparts)[0]
    return density, diag


def solution(mesh):
    placed = (P("col", "pole", None), P("pole", "col", None, None), P(), P())
    return jax.shard_map(
        shards,
        mesh=mesh,
        in_specs=placed,
        out_specs=(P("col", "pole", None), P("col", "pole", None)),
        check_vma=False,
    )
```

```python
import functools

import jax
import jax.numpy as jnp
from jax import lax
from jax.experimental import pallas as pl
from jax.experimental.pallas import tpu as pltpu
from jax.sharding import PartitionSpec as P

F32 = jnp.float32
BF16 = jnp.bfloat16


def dot(a, b):
    return lax.dot_general(a, b, (((1,), (0,)), ((), ())), preferred_element_type=F32)


def dot_t(a, b):
    return lax.dot_general(a, b, (((0,), (0,)), ((), ())), preferred_element_type=F32)


def slot(share, x, t):
    return 2 * x + 2 * share * (t // 2) + t % 2


def kept_rows(source, count, pole, poles, block):
    zero = jnp.zeros((block, block), BF16)
    rows_local = source.shape[0] // block
    return jnp.concatenate(
        [
            lax.select(k * poles + pole < count, source[pl.ds(k * block, block), :], zero)
            for k in range(rows_local)
        ],
        axis=0,
    )


def gram_kernel(poles, share, count_ref, panel_ref, *out_refs):
    pole, col = lax.axis_index("pole"), lax.axis_index("col")
    owned, block = panel_ref.shape[0], panel_ref.shape[2]
    for k, out_ref in enumerate(out_refs):
        for t in range(share):
            i = col ^ slot(share, (pole // 2) ^ k, t)
            x = kept_rows(panel_ref.at[i], count_ref[i * owned + col], pole, poles, block)
            out_ref[t] = dot_t(x, x).astype(BF16)


def turn_kernel(share, inv_ref, *out_refs):
    pole, col = lax.axis_index("pole"), lax.axis_index("col")
    for k, out_ref in enumerate(out_refs):
        for t in range(share):
            out_ref[t] = inv_ref[col ^ slot(share, (pole // 2) ^ k, t)]


def gsum_kernel(share, *refs):
    *got_refs, keep_ref, give_ref = refs
    for t in range(share):
        g = sum(got_ref[t].astype(F32) for got_ref in got_refs).astype(BF16)
        (give_ref if t % 2 else keep_ref)[t // 2] = g


def pair_kernel(a_ref, b_ref, *out_refs):
    for f, out_ref in enumerate(out_refs):
        out_ref[0] = a_ref[f]
        out_ref[1] = b_ref[f]


def gown_kernel(b0_ref, b1_ref, a0_ref, a1_ref, out_ref):
    for f, (x_ref, y_ref) in enumerate(((a0_ref, a1_ref), (b0_ref, b1_ref))):
        out_ref[f] = (x_ref[...].astype(F32) + y_ref[...].astype(F32)).astype(BF16)


def add_kernel(a_ref, b_ref, out_ref):
    out_ref[...] = (a_ref[...].astype(F32) + b_ref[...].astype(F32)).astype(BF16)


def prep_kernel(share, w_ref, count_ref, *refs):
    *got_refs, m_ref, base_ref, gain_ref, wide_ref, flip_ref = refs
    pole, col = lax.axis_index("pole"), lax.axis_index("col")
    block = m_ref.shape[1]
    owned = share * len(got_refs)
    for t in range(share):
        count = count_ref[col * owned + (col ^ slot(share, pole // 2, t))]
        scale = 1.0 / (jnp.full((1, block), block, F32) * count.astype(F32))
        base = jnp.zeros((block, block), F32)
        for k, got_ref in enumerate(got_refs):
            inv = got_ref[t]
            w = w_ref[pole ^ (2 * k)]
            base = base + w * inv.astype(F32)
            gain_ref[t, :, k * block:(k + 1) * block] = w * scale
            wide_ref[t, :, k * block:(k + 1) * block] = inv
            flip_ref[t, :, k * block:(k + 1) * block] = inv.T
        base_ref[t] = base
        m_ref[t] = (-base).astype(BF16)


def diag_kernel(share, base_ref, gain_ref, wide_ref, flip_ref, *refs):
    g_ref, out_ref = refs
    block = base_ref.shape[1]
    half = wide_ref.shape[2] // block
    chunk = out_ref.shape[2]
    for t in range(share):
        g = g_ref[t // 2, t % 2]
        v = dot(g, wide_ref[t]) * gain_ref[t]
        v = jnp.concatenate([v[:, k * block:(k + 1) * block] for k in range(half)], axis=0)
        d = (base_ref[t] + dot(flip_ref[t], v.astype(BF16))).astype(BF16)
        for p in range(out_ref.shape[0]):
            out_ref[p, t] = d[p * chunk:(p + 1) * chunk]


def finish_kernel(share, got_ref, out_ref):
    col = lax.axis_index("col")
    for x in range(got_ref.shape[0] // 2):
        for t in range(share):
            d = got_ref[2 * x, t].astype(F32) + got_ref[2 * x + 1, t].astype(F32)
            out_ref[col ^ slot(share, x, t)] = d.astype(BF16)


def density_kernel(poles, share, count_ref, moved_ref, *refs):
    *m_refs, out_ref = refs
    pole, col = lax.axis_index("pole"), lax.axis_index("col")
    owned, block = moved_ref.shape[0], moved_ref.shape[2]
    for k, m_ref in enumerate(m_refs):
        for t in range(share):
            i = col ^ slot(share, (pole // 2) ^ k, t)
            x = kept_rows(moved_ref.at[i], count_ref[col * owned + i], pole, poles, block)
            out_ref[i] = dot(x, m_ref[t]).astype(BF16)


def shards(panel, pivot_inverse, row_count, pole_weight):
    owned, rows, block = panel.shape
    poles = lax.axis_size("pole")
    cols = lax.axis_size("col")
    pole_at = lax.axis_index("pole")
    col_at = lax.axis_index("col")
    half = poles // 2
    share = owned // half
    chunk = block // poles
    smem = pl.BlockSpec(memory_space=pltpu.SMEM)
    vmem = pl.BlockSpec(memory_space=pltpu.VMEM)
    shape = lambda *s: jax.ShapeDtypeStruct(s, BF16)

    def call(body, name, ins, outs, flops=0):
        moved_bytes = 2 * sum(o.size for o in outs) * 2
        return pl.pallas_call(
            body,
            in_specs=ins,
            out_specs=[vmem] * len(outs),
            out_shape=outs,
            compiler_params=pltpu.CompilerParams(vmem_limit_bytes=32 * 1024 * 1024),
            cost_estimate=pl.CostEstimate(flops=flops, bytes_accessed=moved_bytes, transcendentals=0),
            name=name,
        )

    def swap(x, k):
        return lax.ppermute(x, "pole", [(i, i ^ k) for i in range(poles)])

    moved = lax.all_to_all(panel, "col", 0, 0, tiled=True)

    turned = call(
        functools.partial(turn_kernel, share), "turn", [vmem], [shape(share, block, block)] * half
    )(pivot_inverse[0])
    sent = call(
        functools.partial(gram_kernel, poles, share), "gram",
        [smem, vmem], [shape(share, block, block)] * half,
        2 * owned * rows * block * block,
    )(row_count, panel)
    grams = [sent[0]] + [swap(sent[k], 2 * k) for k in range(1, half)]
    inverses = [turned[0]] + [swap(turned[k], 2 * k) for k in range(1, half)]

    keep, give = call(
        functools.partial(gsum_kernel, share), "gsum", [vmem] * half, [shape(share // 2, block, block)] * 2
    )(*grams)
    near = lax.ppermute(give, "col", [(c, c ^ 1) for c in range(cols)])
    here, side = call(pair_kernel, "pair", [vmem] * 2, [shape(2, block, block)] * 2)(keep, near)

    def shift(x, z, flip):
        pairs = [(p * cols + c, (p ^ z) * cols + (c ^ flip(p))) for p in range(poles) for c in range(cols)]
        return lax.ppermute(x, ("pole", "col"), pairs)

    over = lambda p: 2 * share
    gfull = call(gown_kernel, "gown", [vmem] * 4, [shape(2, 2, block, block)])(
        shift(side, 1, over), shift(side, 0, over), here, swap(here, 1)
    )[0]
    gfull = shift(gfull, 0, lambda p: 2 * (p // 2))

    wide = shape(share, block, half * block)
    mhalf, base, gain, wide, flip = call(
        functools.partial(prep_kernel, share), "prep", [smem] * 2 + [vmem] * half,
        [shape(share, block, block), jax.ShapeDtypeStruct((share, block, block), F32), jax.ShapeDtypeStruct((share, 1, half * block), F32), wide, wide],
    )(pole_weight, row_count, *inverses)
    mfull = call(add_kernel, "weights", [vmem] * 2, [shape(share, block, block)])(mhalf, swap(mhalf, 1))[0]
    mparts = [mfull] + [swap(mfull, 2 * k) for k in range(1, half)]

    part = call(
        functools.partial(diag_kernel, share), "diag",
        [vmem] * 5, [shape(poles, share, chunk, block)],
        6 * owned * block * block * block,
    )(base, gain, wide, flip, gfull)[0]
    part, moved = lax.optimization_barrier((part, moved))
    part = lax.all_to_all(part, "pole", 0, 0, tiled=True)
    diag = call(functools.partial(finish_kernel, share), "finish", [vmem], [shape(owned, chunk, block)])(part)[0]

    density = call(
        functools.partial(density_kernel, poles, share), "density",
        [smem, vmem] + [vmem] * half, [shape(owned, rows, block)],
        2 * owned * rows * block * block,
    )(row_count, moved, *mparts)[0]
    return density, diag


def solution(mesh):
    placed = (P("col", "pole", None), P("pole", "col", None, None), P(), P())
    return jax.shard_map(
        shards,
        mesh=mesh,
        in_specs=placed,
        out_specs=(P("col", "pole", None), P("col", "pole", None)),
        check_vma=False,
    )
```

```python
import functools

import jax
import jax.numpy as jnp
from jax import lax
from jax.experimental import pallas as pl
from jax.experimental.pallas import tpu as pltpu
from jax.sharding import PartitionSpec as P

F32 = jnp.float32
BF16 = jnp.bfloat16


def dot(a, b):
    return lax.dot_general(a, b, (((1,), (0,)), ((), ())), preferred_element_type=F32)


def dot_t(a, b):
    return lax.dot_general(a, b, (((0,), (0,)), ((), ())), preferred_element_type=F32)


def slot(share, x, t):
    return 2 * x + 2 * share * (t // 2) + t % 2


def kept_rows(source, count, pole, poles, block):
    zero = jnp.zeros((block, block), BF16)
    rows_local = source.shape[0] // block
    return jnp.concatenate(
        [
            lax.select(k * poles + pole < count, source[pl.ds(k * block, block), :], zero)
            for k in range(rows_local)
        ],
        axis=0,
    )


def gram_kernel(poles, share, count_ref, panel_ref, *out_refs):
    pole, col = lax.axis_index("pole"), lax.axis_index("col")
    owned, block = panel_ref.shape[0], panel_ref.shape[2]
    for k, out_ref in enumerate(out_refs):
        for t in range(share):
            i = col ^ slot(share, (pole // 2) ^ k, t)
            x = kept_rows(panel_ref.at[i], count_ref[i * owned + col], pole, poles, block)
            out_ref[t] = dot_t(x, x).astype(BF16)


def turn_kernel(share, inv_ref, *out_refs):
    pole, col = lax.axis_index("pole"), lax.axis_index("col")
    for k, out_ref in enumerate(out_refs):
        for t in range(share):
            out_ref[t] = inv_ref[col ^ slot(share, (pole // 2) ^ k, t)]


def gsum_kernel(share, *refs):
    *got_refs, keep_ref, give_ref = refs
    for t in range(share):
        g = sum(got_ref[t].astype(F32) for got_ref in got_refs).astype(BF16)
        (give_ref if t % 2 else keep_ref)[t // 2] = g


def pair_kernel(a_ref, b_ref, *out_refs):
    for f, out_ref in enumerate(out_refs):
        out_ref[0] = a_ref[f]
        out_ref[1] = b_ref[f]


def gown_kernel(b0_ref, b1_ref, a0_ref, a1_ref, out_ref):
    for f, (x_ref, y_ref) in enumerate(((a0_ref, a1_ref), (b0_ref, b1_ref))):
        out_ref[f] = (x_ref[...].astype(F32) + y_ref[...].astype(F32)).astype(BF16)


def add_kernel(a_ref, b_ref, out_ref):
    out_ref[...] = (a_ref[...].astype(F32) + b_ref[...].astype(F32)).astype(BF16)


def prep_kernel(share, w_ref, count_ref, *refs):
    *got_refs, m_ref, base_ref, gain_ref, wide_ref, flip_ref = refs
    pole, col = lax.axis_index("pole"), lax.axis_index("col")
    block = m_ref.shape[1]
    owned = share * len(got_refs)
    for t in range(share):
        count = count_ref[col * owned + (col ^ slot(share, pole // 2, t))]
        scale = 1.0 / (jnp.full((1, block), block, F32) * count.astype(F32))
        base = jnp.zeros((block, block), F32)
        for k, got_ref in enumerate(got_refs):
            inv = got_ref[t]
            w = w_ref[pole ^ (2 * k)]
            base = base + w * inv.astype(F32)
            gain_ref[t, :, k * block:(k + 1) * block] = w * scale
            wide_ref[t, :, k * block:(k + 1) * block] = inv
            flip_ref[t, :, k * block:(k + 1) * block] = inv.T
        base_ref[t] = base
        m_ref[t] = (-base).astype(BF16)


def diag_kernel(share, base_ref, gain_ref, wide_ref, flip_ref, *refs):
    g_ref, out_ref = refs
    block = base_ref.shape[1]
    half = wide_ref.shape[2] // block
    chunk = out_ref.shape[2]
    middle = []
    for t in range(share):
        v = (dot(g_ref[t // 2, t % 2], wide_ref[t]) * gain_ref[t]).astype(BF16)
        middle.append(jnp.concatenate([v[:, k * block:(k + 1) * block] for k in range(half)], axis=0))
    for t, v in enumerate(middle):
        d = (base_ref[t] + dot(flip_ref[t], v)).astype(BF16)
        for p in range(out_ref.shape[0]):
            out_ref[p, t] = d[p * chunk:(p + 1) * chunk]


def finish_kernel(share, got_ref, out_ref):
    col = lax.axis_index("col")
    for x in range(got_ref.shape[0] // 2):
        for t in range(share):
            d = got_ref[2 * x, t].astype(F32) + got_ref[2 * x + 1, t].astype(F32)
            out_ref[col ^ slot(share, x, t)] = d.astype(BF16)


def density_kernel(poles, share, count_ref, moved_ref, *refs):
    *m_refs, out_ref = refs
    pole, col = lax.axis_index("pole"), lax.axis_index("col")
    owned, block = moved_ref.shape[0], moved_ref.shape[2]
    for k, m_ref in enumerate(m_refs):
        for t in range(share):
            i = col ^ slot(share, (pole // 2) ^ k, t)
            x = kept_rows(moved_ref.at[i], count_ref[col * owned + i], pole, poles, block)
            out_ref[i] = dot(x, m_ref[t]).astype(BF16)


def shards(panel, pivot_inverse, row_count, pole_weight):
    owned, rows, block = panel.shape
    poles = lax.axis_size("pole")
    cols = lax.axis_size("col")
    pole_at = lax.axis_index("pole")
    col_at = lax.axis_index("col")
    half = poles // 2
    share = owned // half
    chunk = block // poles
    smem = pl.BlockSpec(memory_space=pltpu.SMEM)
    vmem = pl.BlockSpec(memory_space=pltpu.VMEM)
    shape = lambda *s: jax.ShapeDtypeStruct(s, BF16)

    def call(body, name, ins, outs, flops=0):
        moved_bytes = 2 * sum(o.size for o in outs) * 2
        return pl.pallas_call(
            body,
            in_specs=ins,
            out_specs=[vmem] * len(outs),
            out_shape=outs,
            compiler_params=pltpu.CompilerParams(vmem_limit_bytes=32 * 1024 * 1024),
            cost_estimate=pl.CostEstimate(flops=flops, bytes_accessed=moved_bytes, transcendentals=0),
            name=name,
        )

    def swap(x, k):
        return lax.ppermute(x, "pole", [(i, i ^ k) for i in range(poles)])

    moved = lax.all_to_all(panel, "col", 0, 0, tiled=True)

    turned = call(
        functools.partial(turn_kernel, share), "turn", [vmem], [shape(share, block, block)] * half
    )(pivot_inverse[0])
    sent = call(
        functools.partial(gram_kernel, poles, share), "gram",
        [smem, vmem], [shape(share, block, block)] * half,
        2 * owned * rows * block * block,
    )(row_count, panel)
    grams = [sent[0]] + [swap(sent[k], 2 * k) for k in range(1, half)]
    inverses = [turned[0]] + [swap(turned[k], 2 * k) for k in range(1, half)]

    keep, give = call(
        functools.partial(gsum_kernel, share), "gsum", [vmem] * half, [shape(share // 2, block, block)] * 2
    )(*grams)
    near = lax.ppermute(give, "col", [(c, c ^ 1) for c in range(cols)])
    here, side = call(pair_kernel, "pair", [vmem] * 2, [shape(2, block, block)] * 2)(keep, near)

    def shift(x, z, flip):
        pairs = [(p * cols + c, (p ^ z) * cols + (c ^ flip(p))) for p in range(poles) for c in range(cols)]
        return lax.ppermute(x, ("pole", "col"), pairs)

    over = lambda p: 2 * share
    gfull = call(gown_kernel, "gown", [vmem] * 4, [shape(2, 2, block, block)])(
        shift(side, 1, over), shift(side, 0, over), here, swap(here, 1)
    )[0]
    gfull = shift(gfull, 0, lambda p: 2 * (p // 2))

    wide = shape(share, block, half * block)
    mhalf, base, gain, wide, flip = call(
        functools.partial(prep_kernel, share), "prep", [smem] * 2 + [vmem] * half,
        [shape(share, block, block), jax.ShapeDtypeStruct((share, block, block), F32), jax.ShapeDtypeStruct((share, 1, half * block), F32), wide, wide],
    )(pole_weight, row_count, *inverses)
    mfull = call(add_kernel, "weights", [vmem] * 2, [shape(share, block, block)])(mhalf, swap(mhalf, 1))[0]
    mparts = [mfull] + [swap(mfull, 2 * k) for k in range(1, half)]

    part = call(
        functools.partial(diag_kernel, share), "diag",
        [vmem] * 5, [shape(poles, share, chunk, block)],
        6 * owned * block * block * block,
    )(base, gain, wide, flip, gfull)[0]
    part, moved = lax.optimization_barrier((part, moved))
    part = lax.all_to_all(part, "pole", 0, 0, tiled=True)
    diag = call(functools.partial(finish_kernel, share), "finish", [vmem], [shape(owned, chunk, block)])(part)[0]

    density = call(
        functools.partial(density_kernel, poles, share), "density",
        [smem, vmem] + [vmem] * half, [shape(owned, rows, block)],
        2 * owned * rows * block * block,
    )(row_count, moved, *mparts)[0]
    return density, diag


def solution(mesh):
    placed = (P("col", "pole", None), P("pole", "col", None, None), P(), P())
    return jax.shard_map(
        shards,
        mesh=mesh,
        in_specs=placed,
        out_specs=(P("col", "pole", None), P("col", "pole", None)),
        check_vma=False,
    )
```

```python
import functools

import jax
import jax.numpy as jnp
from jax import lax
from jax.experimental import pallas as pl
from jax.experimental.pallas import tpu as pltpu
from jax.sharding import PartitionSpec as P

F32 = jnp.float32
BF16 = jnp.bfloat16


def dot(a, b):
    return lax.dot_general(a, b, (((1,), (0,)), ((), ())), preferred_element_type=F32)


def dot_t(a, b):
    return lax.dot_general(a, b, (((0,), (0,)), ((), ())), preferred_element_type=F32)


def slot(share, x, t):
    return 2 * x + 2 * share * (t // 2) + t % 2


def kept_rows(source, count, pole, poles, block):
    zero = jnp.zeros((block, block), BF16)
    rows_local = source.shape[0] // block
    return jnp.concatenate(
        [
            lax.select(k * poles + pole < count, source[pl.ds(k * block, block), :], zero)
            for k in range(rows_local)
        ],
        axis=0,
    )


def gram_kernel(poles, share, count_ref, panel_ref, *out_refs):
    pole, col = lax.axis_index("pole"), lax.axis_index("col")
    owned, block = panel_ref.shape[0], panel_ref.shape[2]
    for k, out_ref in enumerate(out_refs):
        for t in range(share):
            i = col ^ slot(share, (pole // 2) ^ k, t)
            x = kept_rows(panel_ref.at[i], count_ref[i * owned + col], pole, poles, block)
            out_ref[t] = dot_t(x, x).astype(BF16)


def turn_kernel(share, inv_ref, *out_refs):
    pole, col = lax.axis_index("pole"), lax.axis_index("col")
    for k, out_ref in enumerate(out_refs):
        for t in range(share):
            out_ref[t] = inv_ref[col ^ slot(share, (pole // 2) ^ k, t)]


def gsum_kernel(share, *refs):
    *got_refs, keep_ref, give_ref = refs
    for t in range(share):
        g = sum(got_ref[t].astype(F32) for got_ref in got_refs).astype(BF16)
        (give_ref if t % 2 else keep_ref)[t // 2] = g


def pair_kernel(a_ref, b_ref, *out_refs):
    for f, out_ref in enumerate(out_refs):
        out_ref[0] = a_ref[f]
        out_ref[1] = b_ref[f]


def gown_kernel(b0_ref, b1_ref, a0_ref, a1_ref, out_ref):
    for f, (x_ref, y_ref) in enumerate(((a0_ref, a1_ref), (b0_ref, b1_ref))):
        out_ref[f] = (x_ref[...].astype(F32) + y_ref[...].astype(F32)).astype(BF16)


def add_kernel(a_ref, b_ref, out_ref):
    out_ref[...] = (a_ref[...].astype(F32) + b_ref[...].astype(F32)).astype(BF16)


def prep_kernel(share, w_ref, count_ref, *refs):
    *got_refs, m_ref, base_ref, gain_ref, wide_ref, flip_ref = refs
    pole, col = lax.axis_index("pole"), lax.axis_index("col")
    block = m_ref.shape[1]
    owned = share * len(got_refs)
    for t in range(share):
        count = count_ref[col * owned + (col ^ slot(share, pole // 2, t))]
        scale = 1.0 / (jnp.full((1, block), block, F32) * count.astype(F32))
        base = jnp.zeros((block, block), F32)
        for k, got_ref in enumerate(got_refs):
            inv = got_ref[t]
            w = w_ref[pole ^ (2 * k)]
            base = base + w * inv.astype(F32)
            gain_ref[t, :, k * block:(k + 1) * block] = w * scale
            wide_ref[t, :, k * block:(k + 1) * block] = inv
            flip_ref[t, :, k * block:(k + 1) * block] = inv.T
        base_ref[t] = base
        m_ref[t] = (-base).astype(BF16)


def diag_kernel(share, base_ref, gain_ref, wide_ref, flip_ref, g_ref, out_ref, rows_ref, done):
    block = base_ref.shape[1]
    half = wide_ref.shape[2] // block
    poles, chunk = rows_ref.shape[1], rows_ref.shape[2]
    copies = []
    middle = []
    for t in range(share):
        v = (dot(g_ref[t // 2, t % 2], wide_ref[t]) * gain_ref[t]).astype(BF16)
        middle.append(jnp.concatenate([v[:, k * block:(k + 1) * block] for k in range(half)], axis=0))
    for t, v in enumerate(middle):
        d = (base_ref[t] + dot(flip_ref[t], v)).astype(BF16)
        for p in range(poles):
            rows_ref[t, p] = d[p * chunk:(p + 1) * chunk]
        copies.append(pltpu.make_async_copy(rows_ref.at[t], out_ref.at[:, t], done.at[t]))
        copies[-1].start()
    for copy in copies:
        copy.wait()


def finish_kernel(share, got_ref, out_ref):
    col = lax.axis_index("col")
    sums = [
        (got_ref[2 * x].astype(F32) + got_ref[2 * x + 1].astype(F32)).astype(BF16) for x in range(got_ref.shape[0] // 2)
    ]
    for x, d in enumerate(sums):
        for t in range(share):
            out_ref[col ^ slot(share, x, t)] = d[t]


def density_kernel(poles, share, count_ref, moved_ref, *refs):
    *m_refs, out_ref = refs
    pole, col = lax.axis_index("pole"), lax.axis_index("col")
    owned, block = moved_ref.shape[0], moved_ref.shape[2]
    for k, m_ref in enumerate(m_refs):
        for t in range(share):
            i = col ^ slot(share, (pole // 2) ^ k, t)
            x = kept_rows(moved_ref.at[i], count_ref[col * owned + i], pole, poles, block)
            out_ref[i] = dot(x, m_ref[t]).astype(BF16)


def shards(panel, pivot_inverse, row_count, pole_weight):
    owned, rows, block = panel.shape
    poles = lax.axis_size("pole")
    cols = lax.axis_size("col")
    pole_at = lax.axis_index("pole")
    col_at = lax.axis_index("col")
    half = poles // 2
    share = owned // half
    chunk = block // poles
    smem = pl.BlockSpec(memory_space=pltpu.SMEM)
    vmem = pl.BlockSpec(memory_space=pltpu.VMEM)
    shape = lambda *s: jax.ShapeDtypeStruct(s, BF16)

    def call(body, name, ins, outs, flops=0):
        moved_bytes = 2 * sum(o.size for o in outs) * 2
        return pl.pallas_call(
            body,
            in_specs=ins,
            out_specs=[vmem] * len(outs),
            out_shape=outs,
            compiler_params=pltpu.CompilerParams(vmem_limit_bytes=32 * 1024 * 1024),
            cost_estimate=pl.CostEstimate(flops=flops, bytes_accessed=moved_bytes, transcendentals=0),
            name=name,
        )

    def swap(x, k):
        return lax.ppermute(x, "pole", [(i, i ^ k) for i in range(poles)])

    moved = lax.all_to_all(panel, "col", 0, 0, tiled=True)

    turned = call(
        functools.partial(turn_kernel, share), "turn", [vmem], [shape(share, block, block)] * half
    )(pivot_inverse[0])
    sent = call(
        functools.partial(gram_kernel, poles, share), "gram",
        [smem, vmem], [shape(share, block, block)] * half,
        2 * owned * rows * block * block,
    )(row_count, panel)
    grams = [sent[0]] + [swap(sent[k], 2 * k) for k in range(1, half)]
    inverses = [turned[0]] + [swap(turned[k], 2 * k) for k in range(1, half)]

    keep, give = call(
        functools.partial(gsum_kernel, share), "gsum", [vmem] * half, [shape(share // 2, block, block)] * 2
    )(*grams)
    near = lax.ppermute(give, "col", [(c, c ^ 1) for c in range(cols)])
    here, side = call(pair_kernel, "pair", [vmem] * 2, [shape(2, block, block)] * 2)(keep, near)

    def shift(x, z, flip):
        pairs = [(p * cols + c, (p ^ z) * cols + (c ^ flip(p))) for p in range(poles) for c in range(cols)]
        return lax.ppermute(x, ("pole", "col"), pairs)

    over = lambda p: 2 * share
    gfull = call(gown_kernel, "gown", [vmem] * 4, [shape(2, 2, block, block)])(
        shift(side, 1, over), shift(side, 0, over), here, swap(here, 1)
    )[0]
    gfull = shift(gfull, 0, lambda p: 2 * (p // 2))

    wide = shape(share, block, half * block)
    mhalf, base, gain, wide, flip = call(
        functools.partial(prep_kernel, share), "prep", [smem] * 2 + [vmem] * half,
        [shape(share, block, block), jax.ShapeDtypeStruct((share, block, block), F32), jax.ShapeDtypeStruct((share, 1, half * block), F32), wide, wide],
    )(pole_weight, row_count, *inverses)
    mfull = call(add_kernel, "weights", [vmem] * 2, [shape(share, block, block)])(mhalf, swap(mhalf, 1))[0]
    mparts = [mfull] + [swap(mfull, 2 * k) for k in range(1, half)]

    part = pl.pallas_call(
        functools.partial(diag_kernel, share),
        in_specs=[vmem] * 5,
        out_specs=pl.BlockSpec(memory_space=pl.ANY),
        out_shape=shape(poles, share, chunk, block),
        scratch_shapes=[pltpu.VMEM((share, poles, chunk, block), BF16), pltpu.SemaphoreType.DMA((share,))],
        compiler_params=pltpu.CompilerParams(vmem_limit_bytes=32 * 1024 * 1024),
        cost_estimate=pl.CostEstimate(
            flops=6 * owned * block * block * block, bytes_accessed=4 * owned * block * block, transcendentals=0
        ),
        name="diag",
    )(base, gain, wide, flip, gfull)
    part, moved = lax.optimization_barrier((part, moved))
    part = lax.all_to_all(part, "pole", 0, 0, tiled=True)
    diag = call(functools.partial(finish_kernel, share), "finish", [vmem], [shape(owned, chunk, block)])(part)[0]

    density = call(
        functools.partial(density_kernel, poles, share), "density",
        [smem, vmem] + [vmem] * half, [shape(owned, rows, block)],
        2 * owned * rows * block * block,
    )(row_count, moved, *mparts)[0]
    return density, diag


def solution(mesh):
    placed = (P("col", "pole", None), P("pole", "col", None, None), P(), P())
    return jax.shard_map(
        shards,
        mesh=mesh,
        in_specs=placed,
        out_specs=(P("col", "pole", None), P("col", "pole", None)),
        check_vma=False,
    )
```
